32 devices in a mesh: ctx: 4 (over x, core), head: 8 (over z, y).
Axes of the slice: x: 2, y: 2, z: 4, core: 2. Of those that a mesh axis runs over, the one named last changes fastest.
Arguments:
- queries: bfloat16 [2048, 16, 128], P('ctx', 'head'), may hold values from -42 to 42
- cached_keys: bfloat16 [1, 16384, 128], P(None, 'ctx'), may hold values from -5 to 5
- cached_values: bfloat16 [1, 16384, 128], P(None, 'ctx'), may hold values from -6 to 6
- grad_out: bfloat16 [2048, 16, 128], P('ctx', 'head'), may hold values from -96 to 96
- chosen: int32 [1, 8, 16], P(None, 'ctx'), may hold values from 0 to 255, as said below
- counts: int32 [1, 8], P(None, 'ctx'), may hold values from 8 to 16, as said below
Outputs:
- grad_query: bfloat16 [2048, 16, 128], P('ctx', 'head')
- grad_keys: bfloat16 [1, 16384, 128], P(None, ('ctx', 'head'))
- grad_values: bfloat16 [1, 16384, 128], P(None, ('ctx', 'head'))
The draws below stay inside these ranges and needn't reach their ends.
Inputs may be any that keep to these rules, and one draw needn't show every extreme that they name: For t < counts[g, b] the entries chosen[g, b, t] are distinct; entries at t >= counts[g, b] are padding. For each group and each run of 2 query blocks starting at a multiple of 2, at most 8 live entries fall in one range of 64 blocks starting at a multiple of 64, and in every group one range receives exactly 8 from every such run. `counts`: in every group some query block has 16 live entries.
All inputs are finite; a program needn't handle non-finite values.
Results may differ from the reference program's by a relative error of at most 0.02.
Values may be sent and summed in bfloat16 or wider, within the bound.
A program may use at most 64 MiB of HBM per device.

```python
import jax
import jax.numpy as jnp
from jax import lax

DH = 128
HPG = 16
KBS = 64
TOPB = 16
QBS = 256
HOT = 4
HEADS = 16
GROUPS = 1
OWNERS = 4
BLK_OWN = 64
KVTOK = 16384
QBLOCKS = 8
QTOK = 2048


def selection(key):
    flow_step = jax.random.fold_in(key, 4049)
    streams = jax.random.split(flow_step, 7)
    hot_owner = jax.random.randint(streams[0], (GROUPS, 1, 1), 0, OWNERS)
    counts = jax.random.randint(streams[1], (GROUPS, QBLOCKS), 8, TOPB + 1)
    full_block = jax.random.randint(streams[2], (GROUPS, 1), 0, QBLOCKS)
    counts = jnp.where(jnp.arange(QBLOCKS)[None, :] == full_block, TOPB, counts)
    offset_draw = jax.random.randint(streams[3], (GROUPS, QBLOCKS, 1), 0, OWNERS - 1)
    base_hot = jax.random.randint(streams[4], (GROUPS, QBLOCKS, 1), 0, BLK_OWN)
    base_other = jax.random.randint(streams[5], (GROUPS, QBLOCKS, 1), 0, BLK_OWN)
    slot_index = jnp.arange(TOPB)[None, None, :]
    rest_rank = slot_index - HOT
    owner_index = jnp.where(slot_index < HOT, hot_owner, (hot_owner + 1 + (rest_rank + offset_draw) % (OWNERS - 1)) % OWNERS)
    local_index = jnp.where(slot_index < HOT, (base_hot + slot_index) % BLK_OWN, (base_other + rest_rank) % BLK_OWN)
    padding = jax.random.randint(streams[6], (GROUPS, QBLOCKS, TOPB), 0, OWNERS * BLK_OWN)
    chosen = jnp.where(slot_index < counts[:, :, None], owner_index * BLK_OWN + local_index, padding)
    return (chosen.astype(jnp.int32), counts.astype(jnp.int32))


def draw_chosen(key, part):
    return selection(key)[0]


def draw_counts(key, part):
    return selection(key)[1]


def draw_cached_keys(key, part):
    flow_step = jax.random.fold_in(key, 811)
    sample = jnp.clip(jax.random.normal(flow_step, (GROUPS, KVTOK, DH), jnp.float32), -5.0, 5.0)
    return sample.astype(jnp.bfloat16)


def draw_queries(key, part):
    flow_step = jax.random.fold_in(key, 977)
    sample = jnp.clip(jax.random.normal(flow_step, (QTOK, HEADS, DH), jnp.float32), -6.0, 6.0)
    return sample.astype(jnp.bfloat16)


def block_levels(key, dims, cuts, least, high):
    def one(position, parts):
        steps = jax.random.uniform(jax.random.fold_in(jax.random.fold_in(key, 6), position), (parts,), jnp.float32, least / len(cuts), high / len(cuts))
        return jnp.repeat(jnp.exp(steps), dims[position] // parts).reshape((-1,) + (1,) * (len(dims) - position - 1))

    level = one(*cuts[0])
    for cut in cuts[1:]:
        level = level * one(*cut)
    return level


def noise(key, shape, width, most, pieces=(), dtype=jnp.bfloat16):
    array = width * jax.random.normal(key, shape, jnp.float32)
    if pieces:
        array = array * block_levels(key, shape, pieces, -0.22, 0.18)
    return jnp.clip(array, -most, most).astype(dtype)


def setup_inputs(seed: int = 0) -> dict:
    splits = jax.random.split(jax.random.key(seed), 7)
    return {
        "queries": draw_queries(jax.random.fold_in(splits[6], 71), 0),
        "cached_keys": draw_cached_keys(jax.random.fold_in(splits[6], 71), 0),
        "cached_values": noise(splits[2], (GROUPS, KVTOK, DH), 1.0, 6.0, ((1, 4),)),
        "grad_out": noise(splits[3], (QTOK, HEADS, DH), 16.0, 96.0, ((0, 4), (1, 8))),
        "chosen": draw_chosen(jax.random.fold_in(splits[6], 71), 0),
        "counts": draw_counts(jax.random.fold_in(splits[6], 71), 0),
    }


def group_pass(queries_g, grad_g, keys_g, values_g, chosen_g, counts_g):
    inv_root = DH ** -0.5
    query_all = queries_g.reshape(QBLOCKS, QBS, HPG, DH)
    grad_all = grad_g.reshape(QBLOCKS, QBS, HPG, DH)

    def visit(totals, inputs):
        grad_k, grad_v = totals
        query_block, grad_block, picked, live_count = inputs
        token_index = (picked[:, None] * KBS + jnp.arange(KBS)[None, :]).reshape(-1).astype(jnp.int32)
        key_rows = keys_g[token_index].astype(jnp.float32)
        value_rows = values_g[token_index].astype(jnp.float32)
        key_live = jnp.repeat(jnp.arange(TOPB) < live_count, KBS)
        live_mask = key_live[None, None, :]
        query_wide = query_block.astype(jnp.float32)
        grad_wide = grad_block.astype(jnp.float32)
        logit_scores = jnp.einsum("qhd,kd->hqk", query_wide, key_rows) * inv_root
        row_peak = jnp.max(jnp.where(live_mask, logit_scores, -jnp.inf), axis=-1, keepdims=True)
        weights_raw = jnp.where(live_mask, jnp.exp(logit_scores - row_peak), 0.0)
        weights = weights_raw / jnp.sum(weights_raw, axis=-1, keepdims=True)
        weight_halves = lax.optimization_barrier(weights.astype(jnp.bfloat16)).astype(jnp.float32)
        attn_out = jnp.einsum("hqk,kd->qhd", weight_halves, value_rows).astype(jnp.bfloat16)
        attn_wide = lax.optimization_barrier(attn_out).astype(jnp.float32)
        row_dot = jnp.transpose(jnp.sum(grad_wide * attn_wide, axis=-1))[:, :, None]
        grad_weights = jnp.einsum("qhd,kd->hqk", grad_wide, value_rows)
        score_gradients = (weights * (grad_weights - row_dot) * inv_root).astype(jnp.bfloat16)
        score_gradients = lax.optimization_barrier(score_gradients).astype(jnp.float32)
        grad_q = jnp.einsum("hqk,kd->qhd", score_gradients, key_rows).astype(jnp.bfloat16)
        slot_dk = jnp.einsum("hqk,qhd->kd", score_gradients, query_wide)
        slot_dv = jnp.einsum("hqk,qhd->kd", weight_halves, grad_wide)
        grad_k = grad_k.at[token_index].add(slot_dk)
        grad_v = grad_v.at[token_index].add(slot_dv)
        return (grad_k, grad_v), grad_q

    empty = jnp.zeros((KVTOK, DH), jnp.float32)
    (grad_k, grad_v), grad_q = lax.scan(visit, (empty, empty), (query_all, grad_all, chosen_g, counts_g))
    return grad_k, grad_v, grad_q.reshape(QTOK, HPG, DH)


def reference(queries, cached_keys, cached_values, grad_out, chosen, counts):
    key_parts = []
    value_parts = []
    query_parts = []
    for group_index in range(GROUPS):
        lower = group_index * HPG
        upper = lower + HPG
        grad_k, grad_v, grad_q = group_pass(queries[:, lower:upper], grad_out[:, lower:upper], cached_keys[group_index], cached_values[group_index], chosen[group_index], counts[group_index])
        key_parts.append(grad_k)
        value_parts.append(grad_v)
        query_parts.append(grad_q)
    grad_query = jnp.concatenate(query_parts, axis=1)
    grad_keys = jnp.stack(key_parts).astype(jnp.bfloat16)
    grad_values = jnp.stack(value_parts).astype(jnp.bfloat16)
    return grad_query, grad_keys, grad_values
```

```python
import functools

import jax
import jax.numpy as jnp
from jax import lax
from jax.experimental import pallas as pl
from jax.experimental.pallas import tpu as pltpu
from jax.sharding import PartitionSpec as P

HPG = 16
KBS = 64
TOPB = 16
QBS = 256
CAP = 8
F32 = jnp.float32
BF16 = jnp.bfloat16


def nt(a, b):
    return lax.dot_general(a, b, (((1,), (1,)), ((), ())), preferred_element_type=F32)


def tn(a, b):
    return lax.dot_general(a, b, (((0,), (0,)), ((), ())), preferred_element_type=F32)


def kernel(
    owners, heads, per_group, groups, runs, head_dev, out_blocks,
    req_s, pos_s, inv_s, cnt_s, req_v, kc, vc, q, do,
    dq, dk_out, dv_out,
    ask_v, ask_s, send_k, send_v, got_k, got_v, sel_k, sel_v,
    weights, halves, scores, rowdot, part, yin, zsend, zin, dsend, gath,
    sem_ask, sem_asks, sem_k, sem_v, sem_y, sem_z, sem_d, sem_e, sem_f,
):
    dh = q.shape[1] // head_dev
    keys = TOPB * KBS
    inv_root = dh ** (-0.5)
    c = lax.axis_index("ctx")
    h = lax.axis_index("head")
    my_group = h // per_group
    lo = h % 2
    far = h // 2
    halves_n = heads // 2
    hi_n = per_group // 2
    hi = (h % per_group) // 2
    other = h + 1 - 2 * lo

    def ctx_peer(d):
        return lax.rem(c + d, owners)

    def far_peer(d):
        return lax.rem(far + d, halves_n) * 2 + lo

    def remote(src, dst, sems, i, where):
        return pltpu.make_async_remote_copy(
            src_ref=src, dst_ref=dst, send_sem=sems.at[0, i], recv_sem=sems.at[1, i],
            device_id=where, device_id_type=pl.DeviceIdType.MESH,
        )

    barrier = pltpu.get_barrier_semaphore()
    peers = [(ctx_peer(d), h) for d in range(1, owners)]
    peers += [(c, far_peer(d)) for d in range(1, halves_n)] + [(c, other)]
    for peer in peers:
        pl.semaphore_signal(barrier, inc=1, device_id=peer, device_id_type=pl.DeviceIdType.MESH)
    pl.semaphore_wait(barrier, len(peers))

    ask = {}
    for d in range(1, owners):
        o = ctx_peer(d)
        ask[d] = remote(req_v.at[o], ask_v.at[c], sem_ask, d, (o, h))
        ask[d].start()
    for k in range(CAP):
        at = req_s[c * groups * CAP + my_group * CAP + k]
        got_k[c, k] = kc[at]
        got_v[c, k] = vc[at]

    kv = {}
    for d in range(owners - 1, 0, -1):
        o = lax.rem(c + owners - d, owners)
        ask[d].wait_recv()
        pltpu.make_async_copy(ask_v.at[o], ask_s.at[o], sem_asks.at[d]).start()
    for d in range(owners - 1, 0, -1):
        o = lax.rem(c + owners - d, owners)
        pltpu.make_async_copy(ask_v.at[o], ask_s.at[o], sem_asks.at[d]).wait()
    for cached, sent, got, sems, name in (
        (kc, send_k, got_k, sem_k, 0), (vc, send_v, got_v, sem_v, 1)
    ):
        for d in range(owners - 1, 0, -1):
            o = lax.rem(c + owners - d, owners)
            for k in range(CAP):
                at = ask_s[o, 0, my_group * CAP + k]
                sent[o, k] = cached[at]
            kv[name, d] = remote(sent.at[o], got.at[c], sems, d, (o, h))
            kv[name, d].start()

    def pick(got, sel, name):
        for d in range(1, owners):
            kv[name, d].wait_recv()
        for b in range(runs):
            for t in range(TOPB):
                at = pos_s[b * TOPB + t]
                sel[b, t * KBS : (t + 1) * KBS, :] = got[at // CAP, at % CAP]

    pick(got_k, sel_k, 0)
    tiles = [(b, e) for b in range(runs) for e in range(head_dev)]

    def rows(ref, b, e):
        return ref[b * QBS : (b + 1) * QBS, e * dh : (e + 1) * dh]

    for b, e in tiles:
        live = lax.broadcasted_iota(jnp.int32, (keys, QBS), 0) < cnt_s[b] * KBS
        s = nt(sel_k[b], rows(q, b, e)) * inv_root
        s = jnp.where(live, s, -jnp.inf)
        w = jnp.exp(s - jnp.max(s, axis=0, keepdims=True))
        w = w * (1.0 / jnp.sum(w, axis=0, keepdims=True))
        weights[b, :, e * QBS : (e + 1) * QBS] = w
        halves[b, :, e * QBS : (e + 1) * QBS] = w.astype(BF16)

    pick(got_v, sel_v, 1)

    def stack(ref, b):
        return jnp.concatenate([rows(ref, b, e) for e in range(head_dev)], axis=0)

    def share(x):
        for k in range(CAP):
            for o in range(owners):
                at = inv_s[o * CAP + k]
                part[x, k % 2, k // 2, o] = scores[x, at]
        cp = remote(part.at[x, 1 - lo], yin.at[x], sem_y, x, (c, other))
        cp.start()
        return cp

    def fold(x, cp):
        cp.wait_recv()
        for i in range(hi_n):
            zsend[x, i] = (part[x, lo, i].astype(F32) + yin[x, i].astype(F32)).astype(BF16)
        out = []
        for d in range(1, hi_n):
            to = lax.rem(hi + d, hi_n)
            z = remote(
                zsend.at[x, to], zin.at[x, d], sem_z, x * hi_n + d,
                (c, my_group * per_group + to * 2 + lo),
            )
            z.start()
            out.append(z)
        return out

    def home(x, zs):
        total = zsend[x, hi].astype(F32)
        for d in range(1, hi_n):
            zs[d - 1].wait_recv()
            total = total + zin[x, d].astype(F32)
        dsend[x] = total.astype(BF16)
        gath[x, lo, far, c] = dsend[x, c]
        out = []
        for d in range(1, owners):
            o = ctx_peer(d)
            cp = remote(dsend.at[x, o], gath.at[x, lo, far, c], sem_d, x * owners + d, (o, h))
            cp.start()
            out.append(cp)
        return out

    def spread(x, ds):
        for cp in ds:
            cp.wait_recv()
        out = []
        mine = gath.at[x, lo, far]
        near = [remote(mine, mine, sem_f, x * halves_n, (c, other))]
        for d in range(1, halves_n):
            cp = remote(mine, mine, sem_e, x * halves_n + d, (c, far_peer(d)))
            cp.start()
            out.append(cp)
        near[0].start()
        return out, near

    def relay(x, es, near):
        for d in range(1, halves_n):
            es[d - 1].wait_recv()
            frm = gath.at[x, lo, lax.rem(far + halves_n - d, halves_n)]
            cp = remote(frm, frm, sem_f, x * halves_n + d, (c, other))
            cp.start()
            near.append(cp)
        for cp in near:
            cp.wait_recv()

    scores[:, runs * TOPB] = jnp.zeros((2, KBS, dh), BF16)
    for b in range(runs):
        dv = jnp.dot(halves[b], stack(do, b), preferred_element_type=F32).astype(BF16)
        scores[0, b * TOPB : (b + 1) * TOPB] = dv.reshape(TOPB, KBS, dh)
    y_v = share(0)
    for b, e in tiles:
        cols = slice(e * QBS, (e + 1) * QBS)
        g = rows(do, b, e)
        attn = tn(sel_v[b], halves[b, :, cols]).astype(BF16).astype(F32)
        rd = jnp.sum(g.astype(F32).T * attn, axis=0, keepdims=True)
        ds = (weights[b, :, cols] * (nt(sel_v[b], g) - rd) * inv_root).astype(BF16)
        halves[b, :, cols] = ds
    z_v = fold(0, y_v)
    for b in range(runs):
        dk = jnp.dot(halves[b], stack(q, b), preferred_element_type=F32).astype(BF16)
        scores[1, b * TOPB : (b + 1) * TOPB] = dk.reshape(TOPB, KBS, dh)
    y_k = share(1)
    d_v = home(0, z_v)
    for b, e in tiles:
        part_q = tn(sel_k[b], halves[b, :, e * QBS : (e + 1) * QBS])
        dq[b * QBS : (b + 1) * QBS, e * dh : (e + 1) * dh] = part_q.T.astype(BF16)
    z_k = fold(1, y_k)
    e_v, n_v = spread(0, d_v)
    d_k = home(1, z_k)
    e_k, n_k = spread(1, d_k)
    relay(0, e_v, n_v)

    def collect(x, out):
        for g in range(groups):
            acc = [jnp.zeros((KBS, dh), F32) for _ in range(out_blocks)]
            for src in range(owners):
                for k in range(CAP):
                    own = req_s[c * groups * CAP + g * CAP + k]
                    at = jnp.where(src == c, own, ask_s[src, 0, g * CAP + k]) - h * out_blocks
                    blk = gath[x, k % 2, g * hi_n + k // 2, src].astype(F32)
                    for j in range(out_blocks):
                        acc[j] = acc[j] + blk * jnp.where(at == j, 1.0, 0.0).astype(F32)
            for j in range(out_blocks):
                out[g, j * KBS : (j + 1) * KBS, :] = acc[j].astype(BF16)

    collect(0, dv_out)
    relay(1, e_k, n_k)
    collect(1, dk_out)

    started = list(ask.values()) + list(kv.values()) + [y_v, y_k] + z_v + z_k + d_v + d_k
    for cp in started + e_v + e_k + n_v + n_k:
        cp.wait_send()


def body(queries, cached_keys, cached_values, grad_out, chosen, counts):
    owners = lax.axis_size("ctx")
    heads = lax.axis_size("head")
    qtok, head_dev, dh = queries.shape
    groups, kv_dev, _ = cached_keys.shape
    blk_own = kv_dev // KBS
    runs = qtok // QBS
    per_group = HPG // head_dev
    my_group = lax.axis_index("head") // per_group
    n = runs * TOPB

    live = (jnp.arange(TOPB)[None, None, :] < counts[:, :, None]).reshape(groups, n)
    flat = chosen.reshape(groups, n)
    owner = flat // blk_own
    local = flat % blk_own
    slot = jnp.arange(n)
    same = (owner[:, :, None] == owner[:, None, :]) & live[:, None, :]
    before = same & (slot[None, None, :] < slot[None, :, None])
    rank = jnp.sum(before.astype(jnp.int32), axis=2)
    position = owner * CAP + rank
    spots = jnp.arange(owners * CAP)
    hit = (position[:, None, :] == spots[None, :, None]) & live[:, None, :]
    req = jnp.sum(jnp.where(hit, local[:, None, :], 0), axis=2)
    inv = n + jnp.sum(jnp.where(hit, slot[None, None, :] - n, 0), axis=2)
    req = req.reshape(groups, owners, CAP).transpose(1, 0, 2).reshape(owners, groups * CAP)
    req_v = jnp.pad(req[:, None, :], ((0, 0), (0, 7), (0, 128 - groups * CAP)))
    position = jnp.where(live, position, 0)

    def mine(a):
        return a[0] if groups == 1 else lax.dynamic_index_in_dim(a, my_group, 0, keepdims=False)

    out_blocks = blk_own // heads
    piece = kv_dev // heads
    smem = pl.BlockSpec(memory_space=pltpu.SMEM)
    vmem = pl.BlockSpec(memory_space=pltpu.VMEM)
    keys = TOPB * KBS
    hi_n = per_group // 2
    block = (KBS, dh)
    dma = pltpu.SemaphoreType.DMA
    dq, dk, dv = pl.pallas_call(
        functools.partial(kernel, owners, heads, per_group, groups, runs, head_dev, out_blocks),
        out_shape=(
            jax.ShapeDtypeStruct((qtok, head_dev * dh), BF16),
            jax.ShapeDtypeStruct((groups, piece, dh), BF16),
            jax.ShapeDtypeStruct((groups, piece, dh), BF16),
        ),
        in_specs=[smem] * 4 + [vmem] * 5,
        out_specs=(vmem, vmem, vmem),
        scratch_shapes=[
            pltpu.VMEM((owners, 8, 128), jnp.int32),
            pltpu.SMEM((owners, 8, 128), jnp.int32),
            pltpu.VMEM((owners, CAP) + block, BF16),
            pltpu.VMEM((owners, CAP) + block, BF16),
            pltpu.VMEM((owners, CAP) + block, BF16),
            pltpu.VMEM((owners, CAP) + block, BF16),
            pltpu.VMEM((runs, keys, dh), BF16),
            pltpu.VMEM((runs, keys, dh), BF16),
            pltpu.VMEM((runs, keys, head_dev * QBS), F32),
            pltpu.VMEM((runs, keys, head_dev * QBS), BF16),
            pltpu.VMEM((2, n + 1) + block, BF16),
            pltpu.VMEM((8, QBS), F32),
            pltpu.VMEM((2, 2, CAP // 2, owners) + block, BF16),
            pltpu.VMEM((2, CAP // 2, owners) + block, BF16),
            pltpu.VMEM((2, CAP // 2, owners) + block, BF16),
            pltpu.VMEM((2, hi_n, owners) + block, BF16),
            pltpu.VMEM((2, owners) + block, BF16),
            pltpu.VMEM((2, 2, heads // 2, owners) + block, BF16),
            dma((2, owners)),
            dma((owners,)),
            dma((2, owners)),
            dma((2, owners)),
            dma((2, 2)),
            dma((2, 2 * hi_n)),
            dma((2, 2 * owners)),
            dma((2, heads)),
            dma((2, heads)),
        ],
        compiler_params=pltpu.CompilerParams(
            collective_id=0, has_side_effects=True, vmem_limit_bytes=48 * 1024 * 1024
        ),
    )(
        req.reshape(-1), mine(position), mine(inv), mine(counts), req_v,
        mine(cached_keys).reshape(blk_own, KBS, dh),
        mine(cached_values).reshape(blk_own, KBS, dh),
        queries.reshape(qtok, head_dev * dh),
        grad_out.reshape(qtok, head_dev * dh),
    )
    return dq.reshape(qtok, head_dev, dh), dk, dv


def solution(mesh):
    return jax.shard_map(
        body,
        mesh=mesh,
        in_specs=(
            P("ctx", "head", None),
            P(None, "ctx", None),
            P(None, "ctx", None),
            P("ctx", "head", None),
            P(None, "ctx", None),
            P(None, "ctx"),
        ),
        out_specs=(
            P("ctx", "head", None),
            P(None, ("ctx", "head"), None),
            P(None, ("ctx", "head"), None),
        ),
        check_vma=False,
    )
```

```python
import functools

import jax
import jax.numpy as jnp
from jax import lax
from jax.experimental import pallas as pl
from jax.experimental.pallas import tpu as pltpu
from jax.sharding import PartitionSpec as P

HPG = 16
KBS = 64
TOPB = 16
QBS = 256
CAP = 8
F32 = jnp.float32
BF16 = jnp.bfloat16


def nt(a, b):
    return lax.dot_general(a, b, (((1,), (1,)), ((), ())), preferred_element_type=F32)


def tn(a, b):
    return lax.dot_general(a, b, (((0,), (0,)), ((), ())), preferred_element_type=F32)


def kernel(
    owners, heads, per_group, groups, runs, head_dev, out_blocks,
    req_s, pos_s, inv_s, cnt_s, req_v, kc_h, vc_h, q_h, do_h,
    dq, dk_out, dv_out,
    kc, vc, q, do,
    ask_v, ask_s, send_k, send_v, got_k, got_v, sel_k, sel_v,
    weights, halves, scores, part, yin, zsend, zin, dsend, gath,
    sem_ask, sem_asks, sem_k, sem_v, sem_y, sem_z, sem_d, sem_e, sem_f, sem_in,
):
    dh = q.shape[1]
    wide = QBS * head_dev
    keys = TOPB * KBS
    inv_root = dh ** (-0.5)
    c = lax.axis_index("ctx")
    h = lax.axis_index("head")
    my_group = h // per_group
    lo = h % 2
    far = h // 2
    halves_n = heads // 2
    hi_n = per_group // 2
    hi = (h % per_group) // 2
    other = h + 1 - 2 * lo

    def ctx_peer(d):
        return lax.rem(c + d, owners)

    def far_peer(d):
        return lax.rem(far + d, halves_n) * 2 + lo

    def remote(src, dst, sems, i, where):
        return pltpu.make_async_remote_copy(
            src_ref=src, dst_ref=dst, send_sem=sems.at[0, i], recv_sem=sems.at[1, i],
            device_id=where, device_id_type=pl.DeviceIdType.MESH,
        )

    pairs = ((kc_h, kc), (q_h, q), (vc_h, vc), (do_h, do))
    loads = [pltpu.make_async_copy(a, b, sem_in.at[i]) for i, (a, b) in enumerate(pairs)]
    for cp in loads:
        cp.start()
    barrier = pltpu.get_barrier_semaphore()
    peers = [(ctx_peer(d), h) for d in range(1, owners)]
    peers += [(c, far_peer(d)) for d in range(1, halves_n)] + [(c, other)]
    for peer in peers:
        pl.semaphore_signal(barrier, inc=1, device_id=peer, device_id_type=pl.DeviceIdType.MESH)
    pl.semaphore_wait(barrier, len(peers))

    ask = {}
    for d in range(1, owners):
        o = ctx_peer(d)
        ask[d] = remote(req_v.at[o], ask_v.at[c], sem_ask, d, (o, h))
        ask[d].start()
    loads[0].wait()
    for k in range(CAP):
        got_k[c, k] = kc[req_s[c, my_group * CAP + k]]

    kv = {}
    for d in range(owners - 1, 0, -1):
        o = lax.rem(c + owners - d, owners)
        ask[d].wait_recv()
        pltpu.make_async_copy(ask_v.at[o], ask_s.at[o], sem_asks.at[d]).start()
    for d in range(owners - 1, 0, -1):
        o = lax.rem(c + owners - d, owners)
        pltpu.make_async_copy(ask_v.at[o], ask_s.at[o], sem_asks.at[d]).wait()
        for k in range(CAP):
            send_k[o, k] = kc[ask_s[o, 0, my_group * CAP + k]]
        kv[0, d] = remote(send_k.at[o], got_k.at[c], sem_k, d, (o, h))
        kv[0, d].start()
    loads[2].wait()
    for d in range(owners - 1, 0, -1):
        o = lax.rem(c + owners - d, owners)
        for k in range(CAP):
            send_v[o, k] = vc[ask_s[o, 0, my_group * CAP + k]]
        kv[1, d] = remote(send_v.at[o], got_v.at[c], sem_v, d, (o, h))
        kv[1, d].start()
    for k in range(CAP):
        got_v[c, k] = vc[req_s[c, my_group * CAP + k]]
    loads[1].wait()
    loads[3].wait()

    def pick(got, sel, name):
        for d in range(1, owners):
            kv[name, d].wait_recv()
        for b in range(runs):
            for t in range(TOPB):
                at = pos_s[b, t]
                sel[b, t * KBS : (t + 1) * KBS, :] = got[at // CAP, at % CAP]

    pick(got_k, sel_k, 0)
    tiles = [(b, e) for b in range(runs) for e in range(head_dev)]

    def rows(ref, b, e):
        at = b * wide + e * QBS
        return ref[at : at + QBS, :]

    order = list(range(1, owners)) + [0]
    y_cp, z_cp, d_cp, e_cp, f_cp = {}, {}, {}, {}, {}

    def share(x):
        for d in order:
            o = ctx_peer(d)
            for k in range(CAP):
                part[x, k % 2, o, k // 2] = scores[x, inv_s[o, k]]
            y_cp[x, d] = remote(
                part.at[x, 1 - lo, o], yin.at[x, d], sem_y, x * owners + d, (c, other)
            )
            y_cp[x, d].start()

    def fold(x):
        for d in order:
            y_cp[x, d].wait_recv()
            for i in range(hi_n):
                both = part[x, lo, ctx_peer(d), i].astype(F32) + yin[x, d, i].astype(F32)
                zsend[x, d, i] = both.astype(BF16)
            for f in range(1, hi_n):
                to = lax.rem(hi + f, hi_n)
                z_cp[x, d, f] = remote(
                    zsend.at[x, d, to], zin.at[x, d, f], sem_z, (x * owners + d) * hi_n + f,
                    (c, my_group * per_group + to * 2 + lo),
                )
                z_cp[x, d, f].start()

    def home(x):
        for d in order:
            total = zsend[x, d, hi].astype(F32)
            for f in range(1, hi_n):
                z_cp[x, d, f].wait_recv()
                total = total + zin[x, d, f].astype(F32)
            if d == 0:
                gath[x, lo, far, c] = total.astype(BF16)
                continue
            o = ctx_peer(d)
            dsend[x, d] = total.astype(BF16)
            d_cp[x, d] = remote(
                dsend.at[x, d], gath.at[x, lo, far, c], sem_d, x * owners + d, (o, h)
            )
            d_cp[x, d].start()

    def spread(x):
        for d in order:
            if d:
                d_cp[x, d].wait_recv()
            src = lax.rem(c + owners - d, owners)
            mine = gath.at[x, lo, far, src]
            at = (x * owners + d) * halves_n
            for f in range(1, halves_n):
                e_cp[x, d, f] = remote(mine, mine, sem_e, at + f, (c, far_peer(f)))
                e_cp[x, d, f].start()
            f_cp[x, d, 0] = remote(mine, mine, sem_f, at, (c, other))
            f_cp[x, d, 0].start()

    def relay(x):
        for d in order:
            src = lax.rem(c + owners - d, owners)
            for f in range(1, halves_n):
                e_cp[x, d, f].wait_recv()
                frm = gath.at[x, lo, lax.rem(far + halves_n - f, halves_n), src]
                at = (x * owners + d) * halves_n + f
                f_cp[x, d, f] = remote(frm, frm, sem_f, at, (c, other))
                f_cp[x, d, f].start()

    def arrived(x):
        for d in order:
            for f in range(halves_n):
                f_cp[x, d, f].wait_recv()

    for b, e in tiles:
        live = lax.broadcasted_iota(jnp.int32, (keys, QBS), 0) < cnt_s[b] * KBS
        s = nt(sel_k[b], rows(q, b, e)) * inv_root
        s = jnp.where(live, s, -jnp.inf)
        w = jnp.exp(s - jnp.max(s, axis=0, keepdims=True))
        w = w * (1.0 / jnp.sum(w, axis=0, keepdims=True))
        weights[b, :, e * QBS : (e + 1) * QBS] = w
        halves[b, :, e * QBS : (e + 1) * QBS] = w.astype(BF16)
    scores[:, runs * TOPB] = jnp.zeros((2, KBS, dh), BF16)

    def partial(x, other_side):
        for b in range(runs):
            side = other_side[b * wide : (b + 1) * wide, :]
            total = jnp.dot(halves[b], side, preferred_element_type=F32).astype(BF16)
            scores[x, b * TOPB : (b + 1) * TOPB] = total.reshape(TOPB, KBS, dh)

    partial(0, do)
    share(0)
    pick(got_v, sel_v, 1)
    for i, (b, e) in enumerate(tiles):
        cols = slice(e * QBS, (e + 1) * QBS)
        g = rows(do, b, e)
        attn = tn(sel_v[b], halves[b, :, cols]).astype(BF16).astype(F32)
        rd = jnp.sum(g.astype(F32).T * attn, axis=0, keepdims=True)
        ds = (weights[b, :, cols] * (nt(sel_v[b], g) - rd) * inv_root).astype(BF16)
        halves[b, :, cols] = ds
        if i == len(tiles) // 2 - 1:
            fold(0)
    partial(1, q)
    share(1)
    home(0)
    for b, e in tiles:
        part_q = tn(sel_k[b], halves[b, :, e * QBS : (e + 1) * QBS])
        at = b * wide + e * QBS
        dq[at : at + QBS, :] = part_q.T.astype(BF16)
    fold(1)
    spread(0)
    home(1)
    relay(0)
    spread(1)
    arrived(0)

    def collect(x, out):
        for g in range(groups):
            acc = [jnp.zeros((KBS, dh), F32) for _ in range(out_blocks)]
            for src in range(owners):
                for k in range(CAP):
                    own = req_s[c, g * CAP + k]
                    at = jnp.where(src == c, own, ask_s[src, 0, g * CAP + k]) - h * out_blocks
                    blk = gath[x, k % 2, g * hi_n + k // 2, src].astype(F32)
                    for j in range(out_blocks):
                        acc[j] = acc[j] + blk * jnp.where(at == j, 1.0, 0.0).astype(F32)
            for j in range(out_blocks):
                out[g, j * KBS : (j + 1) * KBS, :] = acc[j].astype(BF16)

    collect(0, dv_out)
    relay(1)
    arrived(1)
    collect(1, dk_out)

    for group in (ask, kv, y_cp, z_cp, d_cp, e_cp, f_cp):
        for cp in group.values():
            cp.wait_send()


def body(queries, cached_keys, cached_values, grad_out, chosen, counts):
    owners = lax.axis_size("ctx")
    heads = lax.axis_size("head")
    qtok, head_dev, dh = queries.shape
    groups, kv_dev, _ = cached_keys.shape
    blk_own = kv_dev // KBS
    runs = qtok // QBS
    per_group = HPG // head_dev
    my_group = lax.axis_index("head") // per_group
    n = runs * TOPB

    live = jnp.arange(TOPB)[None, None, :] < counts[:, :, None]
    owner = chosen // blk_own
    local = chosen % blk_own
    slot = jnp.arange(runs)[:, None] * TOPB + jnp.arange(TOPB)[None, :]
    same = (owner[:, :, :, None, None] == owner[:, None, None]) & live[:, None, None]
    before = same & (slot[None, None, None] < slot[None, :, :, None, None])
    rank = jnp.sum(before.astype(jnp.int32), axis=(3, 4))
    position = jnp.where(live, owner * CAP + rank, -1)
    spots = jnp.arange(owners)[:, None] * CAP + jnp.arange(CAP)[None, :]
    hit = position[:, None, None] == spots[None, :, :, None, None]
    req = jnp.sum(jnp.where(hit, local[:, None, None], 0), axis=(3, 4))
    inv = n + jnp.sum(jnp.where(hit, slot[None, None, None] - n, 0), axis=(3, 4))
    req = req.transpose(1, 0, 2).reshape(owners, groups * CAP)
    req_v = jnp.pad(req[:, None, :], ((0, 0), (0, 7), (0, 128 - groups * CAP)))
    position = jnp.maximum(position, 0)

    def mine(a):
        return a[0] if groups == 1 else lax.dynamic_index_in_dim(a, my_group, 0, keepdims=False)

    out_blocks = blk_own // heads
    piece = kv_dev // heads
    smem = pl.BlockSpec(memory_space=pltpu.SMEM)
    vmem = pl.BlockSpec(memory_space=pltpu.VMEM)
    hbm = pl.BlockSpec(memory_space=pl.ANY)
    keys = TOPB * KBS
    hi_n = per_group // 2
    block = (KBS, dh)
    dma = pltpu.SemaphoreType.DMA
    dq, dk, dv = pl.pallas_call(
        functools.partial(kernel, owners, heads, per_group, groups, runs, head_dev, out_blocks),
        out_shape=(
            jax.ShapeDtypeStruct((qtok * head_dev, dh), BF16),
            jax.ShapeDtypeStruct((groups, piece, dh), BF16),
            jax.ShapeDtypeStruct((groups, piece, dh), BF16),
        ),
        in_specs=[smem] * 4 + [vmem] + [hbm] * 4,
        out_specs=(vmem, vmem, vmem),
        scratch_shapes=[
            pltpu.VMEM((blk_own,) + block, BF16),
            pltpu.VMEM((blk_own,) + block, BF16),
            pltpu.VMEM((qtok * head_dev, dh), BF16),
            pltpu.VMEM((qtok * head_dev, dh), BF16),
            pltpu.VMEM((owners, 8, 128), jnp.int32),
            pltpu.SMEM((owners, 8, 128), jnp.int32),
            pltpu.VMEM((owners, CAP) + block, BF16),
            pltpu.VMEM((owners, CAP) + block, BF16),
            pltpu.VMEM((owners, CAP) + block, BF16),
            pltpu.VMEM((owners, CAP) + block, BF16),
            pltpu.VMEM((runs, keys, dh), BF16),
            pltpu.VMEM((runs, keys, dh), BF16),
            pltpu.VMEM((runs, keys, head_dev * QBS), F32),
            pltpu.VMEM((runs, keys, head_dev * QBS), BF16),
            pltpu.VMEM((2, n + 1) + block, BF16),
            pltpu.VMEM((2, 2, owners, CAP // 2) + block, BF16),
            pltpu.VMEM((2, owners, CAP // 2) + block, BF16),
            pltpu.VMEM((2, owners, CAP // 2) + block, BF16),
            pltpu.VMEM((2, owners, hi_n) + block, BF16),
            pltpu.VMEM((2, owners) + block, BF16),
            pltpu.VMEM((2, 2, heads // 2, owners) + block, BF16),
            dma((2, owners)),
            dma((owners,)),
            dma((2, owners)),
            dma((2, owners)),
            dma((2, 2 * owners)),
            dma((2, 2 * owners * hi_n)),
            dma((2, 2 * owners)),
            dma((2, owners * heads)),
            dma((2, owners * heads)),
            dma((4,)),
        ],
        compiler_params=pltpu.CompilerParams(
            collective_id=0, has_side_effects=True, vmem_limit_bytes=60 * 1024 * 1024
        ),
    )(
        req, mine(position), mine(inv), mine(counts), req_v,
        mine(cached_keys).reshape(blk_own, KBS, dh),
        mine(cached_values).reshape(blk_own, KBS, dh),
        queries.reshape(qtok * head_dev, dh),
        grad_out.reshape(qtok * head_dev, dh),
    )
    return dq.reshape(qtok, head_dev, dh), dk, dv


def solution(mesh):
    return jax.shard_map(
        body,
        mesh=mesh,
        in_specs=(
            P("ctx", "head", None),
            P(None, "ctx", None),
            P(None, "ctx", None),
            P("ctx", "head", None),
            P(None, "ctx", None),
            P(None, "ctx"),
        ),
        out_specs=(
            P("ctx", "head", None),
            P(None, ("ctx", "head"), None),
            P(None, ("ctx", "head"), None),
        ),
        check_vma=False,
    )
```

```python
import functools

import jax
import jax.numpy as jnp
from jax import lax
from jax.experimental import pallas as pl
from jax.experimental.pallas import tpu as pltpu
from jax.sharding import PartitionSpec as P

HPG = 16
KBS = 64
TOPB = 16
QBS = 256
CAP = 8
F32 = jnp.float32
BF16 = jnp.bfloat16


def nt(a, b):
    return lax.dot_general(a, b, (((1,), (1,)), ((), ())), preferred_element_type=F32)


def tn(a, b):
    return lax.dot_general(a, b, (((0,), (0,)), ((), ())), preferred_element_type=F32)


def kernel(
    owners, heads, per_group, groups, runs, head_dev, out_blocks,
    req_s, pos_s, inv_s, cnt_s, req_v, kc_h, vc_h, q_h, do_h,
    dq, dk_out, dv_out,
    kc, vc, q, do,
    ask_v, ask_s, send_k, send_v, got_k, got_v, sel_k, sel_v,
    weights, halves, scores, part, yin, zsend, zin, dsend, gath,
    sem_ask, sem_asks, sem_k, sem_v, sem_y, sem_z, sem_d, sem_e, sem_f, sem_in,
):
    dh = q.shape[1]
    wide = QBS * head_dev
    keys = TOPB * KBS
    inv_root = dh ** (-0.5)
    c = lax.axis_index("ctx")
    h = lax.axis_index("head")
    my_group = h // per_group
    lo = h % 2
    far = h // 2
    halves_n = heads // 2
    hi_n = per_group // 2
    hi = (h % per_group) // 2
    other = h + 1 - 2 * lo

    def ctx_peer(d):
        return lax.rem(c + d, owners)

    def far_peer(d):
        return lax.rem(far + d, halves_n) * 2 + lo

    def remote(src, dst, sems, i, where):
        return pltpu.make_async_remote_copy(
            src_ref=src, dst_ref=dst, send_sem=sems.at[0, i], recv_sem=sems.at[1, i],
            device_id=where, device_id_type=pl.DeviceIdType.MESH,
        )

    pairs = ((kc_h, kc), (q_h, q), (vc_h, vc), (do_h, do))
    loads = [pltpu.make_async_copy(a, b, sem_in.at[i]) for i, (a, b) in enumerate(pairs)]
    for cp in loads:
        cp.start()
    barrier = pltpu.get_barrier_semaphore()
    peers = [(ctx_peer(d), h) for d in range(1, owners)]
    peers += [(c, far_peer(d)) for d in range(1, halves_n)] + [(c, other)]
    for peer in peers:
        pl.semaphore_signal(barrier, inc=1, device_id=peer, device_id_type=pl.DeviceIdType.MESH)
    pl.semaphore_wait(barrier, len(peers))

    ask = {}
    for d in range(1, owners):
        o = ctx_peer(d)
        ask[d] = remote(req_v.at[o], ask_v.at[c], sem_ask, d, (o, h))
        ask[d].start()
    loads[0].wait()
    for k in range(CAP):
        got_k[c, k] = kc[req_s[c, my_group * CAP + k]]

    kv = {}
    for d in range(owners - 1, 0, -1):
        o = lax.rem(c + owners - d, owners)
        ask[d].wait_recv()
        pltpu.make_async_copy(ask_v.at[o], ask_s.at[o], sem_asks.at[d]).start()
    for d in range(owners - 1, 0, -1):
        o = lax.rem(c + owners - d, owners)
        pltpu.make_async_copy(ask_v.at[o], ask_s.at[o], sem_asks.at[d]).wait()
        for k in range(CAP):
            send_k[o, k] = kc[ask_s[o, 0, my_group * CAP + k]]
        kv[0, d] = remote(send_k.at[o], got_k.at[c], sem_k, d, (o, h))
        kv[0, d].start()
    loads[2].wait()
    for d in range(owners - 1, 0, -1):
        o = lax.rem(c + owners - d, owners)
        for k in range(CAP):
            send_v[o, k] = vc[ask_s[o, 0, my_group * CAP + k]]
        kv[1, d] = remote(send_v.at[o], got_v.at[c], sem_v, d, (o, h))
        kv[1, d].start()
    for k in range(CAP):
        got_v[c, k] = vc[req_s[c, my_group * CAP + k]]
    loads[1].wait()
    loads[3].wait()

    def pick(got, sel, name):
        for d in range(1, owners):
            kv[name, d].wait_recv()
        for b in range(runs):
            for t in range(TOPB):
                at = pos_s[b, t]
                sel[b, t * KBS : (t + 1) * KBS, :] = got[at // CAP, at % CAP]

    pick(got_k, sel_k, 0)
    tiles = [(b, e) for b in range(runs) for e in range(head_dev)]

    def rows(ref, b, e):
        at = b * wide + e * QBS
        return ref[at : at + QBS, :]

    order = list(range(1, owners)) + [0]
    y_cp, z_cp, d_cp, e_cp, f_cp = {}, {}, {}, {}, {}

    def share(x):
        for d in order:
            o = ctx_peer(d)
            for k in range(CAP):
                part[x, k % 2, o, k // 2] = scores[x, inv_s[o, k]]
            y_cp[x, d] = remote(
                part.at[x, 1 - lo, o], yin.at[x, d], sem_y, x * owners + d, (c, other)
            )
            y_cp[x, d].start()

    def fold(x, d):
        y_cp[x, d].wait_recv()
        for i in range(hi_n):
            both = part[x, lo, ctx_peer(d), i].astype(F32) + yin[x, d, i].astype(F32)
            zsend[x, d, i] = both.astype(BF16)
        for f in range(1, hi_n):
            to = lax.rem(hi + f, hi_n)
            z_cp[x, d, f] = remote(
                zsend.at[x, d, to], zin.at[x, d, f], sem_z, (x * owners + d) * hi_n + f,
                (c, my_group * per_group + to * 2 + lo),
            )
            z_cp[x, d, f].start()

    def home(x, d):
        total = zsend[x, d, hi].astype(F32)
        for f in range(1, hi_n):
            z_cp[x, d, f].wait_recv()
            total = total + zin[x, d, f].astype(F32)
        if d == 0:
            gath[x, lo, far, c] = total.astype(BF16)
            return
        o = ctx_peer(d)
        dsend[x, d] = total.astype(BF16)
        d_cp[x, d] = remote(
            dsend.at[x, d], gath.at[x, lo, far, c], sem_d, x * owners + d, (o, h)
        )
        d_cp[x, d].start()

    def spread(x, d):
        if d:
            d_cp[x, d].wait_recv()
        src = lax.rem(c + owners - d, owners)
        mine = gath.at[x, lo, far, src]
        at = (x * owners + d) * halves_n
        for f in range(1, halves_n):
            e_cp[x, d, f] = remote(mine, mine, sem_e, at + f, (c, far_peer(f)))
            e_cp[x, d, f].start()
        f_cp[x, d, 0] = remote(mine, mine, sem_f, at, (c, other))
        f_cp[x, d, 0].start()

    def relay(x, d):
        src = lax.rem(c + owners - d, owners)
        for f in range(1, halves_n):
            e_cp[x, d, f].wait_recv()
            frm = gath.at[x, lo, lax.rem(far + halves_n - f, halves_n), src]
            at = (x * owners + d) * halves_n + f
            f_cp[x, d, f] = remote(frm, frm, sem_f, at, (c, other))
            f_cp[x, d, f].start()

    def arrived(x):
        for d in order:
            for f in range(halves_n):
                f_cp[x, d, f].wait_recv()

    for b, e in tiles:
        live = lax.broadcasted_iota(jnp.int32, (keys, QBS), 0) < cnt_s[b] * KBS
        s = nt(sel_k[b], rows(q, b, e)) * inv_root
        s = jnp.where(live, s, -jnp.inf)
        w = jnp.exp(s - jnp.max(s, axis=0, keepdims=True))
        w = w * (1.0 / jnp.sum(w, axis=0, keepdims=True))
        weights[b, :, e * QBS : (e + 1) * QBS] = w
        halves[b, :, e * QBS : (e + 1) * QBS] = w.astype(BF16)
    scores[:, runs * TOPB] = jnp.zeros((2, KBS, dh), BF16)

    def partial(x, other_side):
        for b in range(runs):
            side = other_side[b * wide : (b + 1) * wide, :]
            total = jnp.dot(halves[b], side, preferred_element_type=F32).astype(BF16)
            scores[x, b * TOPB : (b + 1) * TOPB] = total.reshape(TOPB, KBS, dh)

    partial(0, do)
    share(0)
    pick(got_v, sel_v, 1)
    for i, (b, e) in enumerate(tiles):
        cols = slice(e * QBS, (e + 1) * QBS)
        g = rows(do, b, e)
        attn = tn(sel_v[b], halves[b, :, cols]).astype(BF16).astype(F32)
        rd = jnp.sum(g.astype(F32).T * attn, axis=0, keepdims=True)
        ds = (weights[b, :, cols] * (nt(sel_v[b], g) - rd) * inv_root).astype(BF16)
        halves[b, :, cols] = ds
        for d in order[owners * i // len(tiles) : owners * (i + 1) // len(tiles)]:
            fold(0, d)
    partial(1, q)
    share(1)
    for d in order:
        home(0, d)
    for b, e in tiles:
        part_q = tn(sel_k[b], halves[b, :, e * QBS : (e + 1) * QBS])
        at = b * wide + e * QBS
        dq[at : at + QBS, :] = part_q.T
    for d in order:
        spread(0, d)
        fold(1, d)
    for d in order:
        home(1, d)
        relay(0, d)
    for d in order:
        spread(1, d)

    def collect(x, out):
        for g in range(groups):
            for first in range(0, out_blocks, 4):
                some = range(first, min(first + 4, out_blocks))
                acc = [jnp.zeros((KBS, dh), F32) for _ in some]
                for src in range(owners):
                    for k in range(CAP):
                        own = req_s[c, g * CAP + k]
                        at = jnp.where(src == c, own, ask_s[src, 0, g * CAP + k]) - h * out_blocks
                        blk = gath[x, k % 2, g * hi_n + k // 2, src].astype(F32)
                        for i, j in enumerate(some):
                            acc[i] = acc[i] + blk * jnp.where(at == j, 1.0, 0.0).astype(F32)
                for i, j in enumerate(some):
                    out[g, j * KBS : (j + 1) * KBS, :] = acc[i]

    arrived(0)
    collect(0, dv_out)
    for d in order:
        relay(1, d)
    arrived(1)
    collect(1, dk_out)

    for group in (ask, kv, y_cp, z_cp, d_cp, e_cp, f_cp):
        for cp in group.values():
            cp.wait_send()


def body(queries, cached_keys, cached_values, grad_out, chosen, counts):
    owners = lax.axis_size("ctx")
    heads = lax.axis_size("head")
    qtok, head_dev, dh = queries.shape
    groups, kv_dev, _ = cached_keys.shape
    blk_own = kv_dev // KBS
    runs = qtok // QBS
    per_group = HPG // head_dev
    my_group = lax.axis_index("head") // per_group
    n = runs * TOPB

    live = jnp.arange(TOPB)[None, None, :] < counts[:, :, None]
    owner = chosen // blk_own
    local = chosen % blk_own
    slot = jnp.arange(runs)[:, None] * TOPB + jnp.arange(TOPB)[None, :]
    same = (owner[:, :, :, None, None] == owner[:, None, None]) & live[:, None, None]
    before = same & (slot[None, None, None] < slot[None, :, :, None, None])
    rank = jnp.sum(before.astype(jnp.int32), axis=(3, 4))
    position = jnp.where(live, owner * CAP + rank, -1)
    spots = jnp.arange(owners)[:, None] * CAP + jnp.arange(CAP)[None, :]
    hit = position[:, None, None] == spots[None, :, :, None, None]
    req = jnp.sum(jnp.where(hit, local[:, None, None], 0), axis=(3, 4))
    inv = n + jnp.sum(jnp.where(hit, slot[None, None, None] - n, 0), axis=(3, 4))
    req = req.transpose(1, 0, 2).reshape(owners, groups * CAP)
    req_v = jnp.pad(req[:, None, :], ((0, 0), (0, 7), (0, 128 - groups * CAP)))
    position = jnp.maximum(position, 0)

    def mine(a):
        return a[0] if groups == 1 else lax.dynamic_index_in_dim(a, my_group, 0, keepdims=False)

    out_blocks = blk_own // heads
    piece = kv_dev // heads
    smem = pl.BlockSpec(memory_space=pltpu.SMEM)
    vmem = pl.BlockSpec(memory_space=pltpu.VMEM)
    hbm = pl.BlockSpec(memory_space=pl.ANY)
    keys = TOPB * KBS
    hi_n = per_group // 2
    block = (KBS, dh)
    dma = pltpu.SemaphoreType.DMA
    dq, dk, dv = pl.pallas_call(
        functools.partial(kernel, owners, heads, per_group, groups, runs, head_dev, out_blocks),
        out_shape=(
            jax.ShapeDtypeStruct((qtok * head_dev, dh), F32),
            jax.ShapeDtypeStruct((groups, piece, dh), F32),
            jax.ShapeDtypeStruct((groups, piece, dh), F32),
        ),
        in_specs=[smem] * 4 + [vmem] + [hbm] * 4,
        out_specs=(vmem, vmem, vmem),
        scratch_shapes=[
            pltpu.VMEM((blk_own,) + block, BF16),
            pltpu.VMEM((blk_own,) + block, BF16),
            pltpu.VMEM((qtok * head_dev, dh), BF16),
            pltpu.VMEM((qtok * head_dev, dh), BF16),
            pltpu.VMEM((owners, 8, 128), jnp.int32),
            pltpu.SMEM((owners, 8, 128), jnp.int32),
            pltpu.VMEM((owners, CAP) + block, BF16),
            pltpu.VMEM((owners, CAP) + block, BF16),
            pltpu.VMEM((owners, CAP) + block, BF16),
            pltpu.VMEM((owners, CAP) + block, BF16),
            pltpu.VMEM((runs, keys, dh), BF16),
            pltpu.VMEM((runs, keys, dh), BF16),
            pltpu.VMEM((runs, keys, head_dev * QBS), F32),
            pltpu.VMEM((runs, keys, head_dev * QBS), BF16),
            pltpu.VMEM((2, n + 1) + block, BF16),
            pltpu.VMEM((2, 2, owners, CAP // 2) + block, BF16),
            pltpu.VMEM((2, owners, CAP // 2) + block, BF16),
            pltpu.VMEM((2, owners, CAP // 2) + block, BF16),
            pltpu.VMEM((2, owners, hi_n) + block, BF16),
            pltpu.VMEM((2, owners) + block, BF16),
            pltpu.VMEM((2, 2, heads // 2, owners) + block, BF16),
            dma((2, owners)),
            dma((owners,)),
            dma((2, owners)),
            dma((2, owners)),
            dma((2, 2 * owners)),
            dma((2, 2 * owners * hi_n)),
            dma((2, 2 * owners)),
            dma((2, owners * heads)),
            dma((2, owners * heads)),
            dma((4,)),
        ],
        compiler_params=pltpu.CompilerParams(
            collective_id=0, has_side_effects=True, vmem_limit_bytes=60 * 1024 * 1024
        ),
    )(
        req, mine(position), mine(inv), mine(counts), req_v,
        mine(cached_keys).reshape(blk_own, KBS, dh),
        mine(cached_values).reshape(blk_own, KBS, dh),
        queries.reshape(qtok * head_dev, dh),
        grad_out.reshape(qtok * head_dev, dh),
    )
    return dq.astype(BF16).reshape(qtok, head_dev, dh), dk.astype(BF16), dv.astype(BF16)


def solution(mesh):
    return jax.shard_map(
        body,
        mesh=mesh,
        in_specs=(
            P("ctx", "head", None),
            P(None, "ctx", None),
            P(None, "ctx", None),
            P("ctx", "head", None),
            P(None, "ctx", None),
            P(None, "ctx"),
        ),
        out_specs=(
            P("ctx", "head", None),
            P(None, ("ctx", "head"), None),
            P(None, ("ctx", "head"), None),
        ),
        check_vma=False,
    )
```
